32 devices in a mesh: row: 4 (over z), col: 8 (over y, x, core).
Axes of the slice: x: 2, y: 2, z: 4, core: 2. Of those that a mesh axis runs over, the one named last changes fastest.
Arguments:
- panel_blocks: bfloat16 [8, 8, 512, 512], P('col', None, 'row'), may hold values from -0.25 to 0.25
- factor_inverse: bfloat16 [8, 512, 512], P('col')
- target_rows: int32 [8, 8], replicated, may hold values from 0 to 7, as said below
- owner_order: int32 [8], replicated, may hold values from 0 to 7, each once
- ancestor_rows: float32 [8, 512, 4096], P('col', 'row'), may hold values from -1.8 to 1.8
Outputs:
- updated_rows: float32 [8, 512, 4096], P('col', 'row')
The draws below stay inside these ranges and needn't reach their ends.
Inputs may be any that keep to these rules, and one draw needn't show every extreme that they name: `target_rows`: each row names 8 different ancestor block rows in ascending order; each index of col holds exactly one supernode. `owner_order`: each ancestor block row once.
All inputs are finite; a program needn't handle non-finite values.
Results may differ from the reference program's by a relative error of at most 0.0024.
Values may be sent and summed in bfloat16 or wider, within the bound.
No kernel may reach another device: no remote copies, remote signals or barrier semaphores. Data moves between devices by JAX's collectives and lax.ppermute only.
A program may use at most 192 MiB of HBM per device.

```python
import math
import jax
import jax.numpy as jnp
from jax import lax

W = 512
PB = 8
SN_DEV = 1
NSUP = 8
NA = 8


def draw_factor_inverse(key, part):
    first_key, second_key = jax.random.split(key)
    shape_full = (NSUP, W, W)
    lower = jax.random.normal(first_key, shape_full, jnp.float32)
    diagonal = jax.random.uniform(second_key, (NSUP, W, 1), jnp.float32, 0.5, 1.5)
    lower = lower * (1.0 / math.sqrt(W))
    row_index = lax.broadcasted_iota(jnp.int32, shape_full, 1)
    col_index = lax.broadcasted_iota(jnp.int32, shape_full, 2)
    result = jnp.where(row_index > col_index, lower, jnp.where(row_index == col_index, diagonal, 0.0))
    return result.astype(jnp.bfloat16)


def draw_target_rows(key, part):
    groups = NSUP // SN_DEV
    group_keys = jax.random.split(key, groups)
    orders = jax.vmap(lambda k: jax.random.permutation(k, NA))(group_keys)
    member = lax.broadcasted_iota(jnp.int32, (SN_DEV, PB), 0)
    within = lax.broadcasted_iota(jnp.int32, (SN_DEV, PB), 1)
    places = (member * PB + within) % NA
    picked = orders[:, places]
    picked = jnp.sort(picked, axis=2)
    return picked.reshape(NSUP, PB).astype(jnp.int32)


def shard_levels(own_key, extent, cuts, least, high):
    level, own = 1.0, jax.random.fold_in(own_key, 6)
    for position, blocks in cuts:
        steps = jnp.exp(jax.random.uniform(jax.random.fold_in(own, position), (blocks,), jnp.float32, least / len(cuts), high / len(cuts)))
        level = level * jnp.repeat(steps, extent[position] // blocks).reshape([-1 if axis == position else 1 for axis in range(len(extent))])
    return level


def bell_draw(key, extent, deviation, reach, cuts=(), held_as=jnp.bfloat16):
    array = deviation * jax.random.normal(key, extent, jnp.float32)
    if cuts:
        array = array * shard_levels(key, extent, cuts, -0.22, 0.18)
    return jnp.clip(array, -reach, reach).astype(held_as)


def setup_inputs(seed: int = 0) -> dict:
    streams_of = jax.random.split(jax.random.key(seed), 6)
    panel_blocks = bell_draw(streams_of[0], (NSUP, PB, W, W), W ** -0.5, 0.25, ((0, 8), (2, 4)))
    factor_inverse = draw_factor_inverse(jax.random.fold_in(streams_of[5], 71), 0)
    target_rows = draw_target_rows(jax.random.fold_in(streams_of[5], 71), 0)
    owner_order = jax.random.permutation(streams_of[3], NA).astype(jnp.int32)
    ancestor_rows = bell_draw(streams_of[4], (NA, W, NA * W), 0.3, 1.8, ((0, 8), (1, 4)), jnp.float32)
    return {"panel_blocks": panel_blocks, "factor_inverse": factor_inverse, "target_rows": target_rows, "owner_order": owner_order, "ancestor_rows": ancestor_rows}


def reference(panel_blocks, factor_inverse, target_rows, owner_order, ancestor_rows):
    def one_supernode(carry, inputs):
        blocks, inverse, targets = inputs
        solved = jnp.einsum('piw,vw->piv', blocks.astype(jnp.float32), inverse.astype(jnp.float32)).astype(jnp.bfloat16)
        solved_wide = solved.astype(jnp.float32)
        product = jnp.einsum('piw,qmw->piqm', solved_wide, solved_wide).astype(jnp.bfloat16)
        product = lax.optimization_barrier(product).astype(jnp.float32)
        carry = carry.at[targets[:, None], :, targets[None, :], :].add(jnp.transpose(product, (0, 2, 1, 3)))
        return carry, None

    zeros_init = jnp.zeros((NA, W, NA, W), jnp.float32)
    update, _ = lax.scan(one_supernode, zeros_init, (panel_blocks, factor_inverse, target_rows))
    ordered = update[owner_order].reshape(NA, W, NA * W)
    return ancestor_rows - ordered
```

```python
import functools

import jax
import jax.numpy as jnp
from jax import lax
from jax.experimental import pallas as pl
from jax.experimental.pallas import tpu as pltpu
from jax.sharding import PartitionSpec as P

BF16 = jnp.bfloat16
F32 = jnp.float32
VMEM_LIMIT = 40 * 1024 * 1024


def solve_rows(blocks, factor_inverse):
    return jnp.einsum(
        "spiw,svw->spiv", blocks, factor_inverse, preferred_element_type=jnp.float32
    ).astype(jnp.bfloat16)


def pick_rows(products, own_targets, order_part):
    matched = own_targets[None, :, :] == order_part[:, None, None]
    places = lax.broadcasted_iota(jnp.int32, matched.shape, 2)
    position = jnp.sum(jnp.where(matched, places, 0), axis=2)
    present = jnp.any(matched, axis=2)
    supernode_ids = lax.broadcasted_iota(jnp.int32, position.shape, 1)
    chosen = products[supernode_ids, position]
    return jnp.where(present[:, :, None, None, None], chosen, jnp.zeros((), chosen.dtype))


def slot_select(targets, order_part, slot_count):
    matched = targets[None, :, :] == order_part[:, None, None]
    present = jnp.any(matched, axis=2)
    rank = jnp.cumsum(present.astype(jnp.int32), axis=1) - 1
    slot_ids = lax.broadcasted_iota(jnp.int32, (1, slot_count, 1), 1)
    selected = present[:, None, :] & (rank[:, None, :] == slot_ids)
    return selected.astype(jnp.float32)


def general_body(panel_blocks, factor_inverse, target_rows, owner_order, ancestor_rows):
    supernodes = panel_blocks.shape[0]
    panel_count = panel_blocks.shape[1]
    own_height = panel_blocks.shape[2]
    width = panel_blocks.shape[3]
    ancestors = owner_order.shape[0]
    col_devices = lax.axis_size("col")
    col_place = lax.axis_index("col")
    own_targets = lax.dynamic_slice_in_dim(target_rows, col_place * supernodes, supernodes, 0)
    own_solved = solve_rows(panel_blocks, factor_inverse)
    products = jnp.einsum(
        "spiw,sqmw->spiqm",
        own_solved,
        lax.all_gather(own_solved, "row", axis=2, tiled=True),
        preferred_element_type=jnp.float32,
    ).astype(jnp.bfloat16)
    block_ids = lax.broadcasted_iota(jnp.int32, (1, 1, 1, ancestors), 3)
    slot_count = (supernodes * panel_count + ancestors - 1) // ancestors
    chosen = pick_rows(products, own_targets, owner_order)
    own_select = slot_select(own_targets, owner_order, slot_count).astype(jnp.bfloat16)
    outgoing = jnp.einsum(
        "jas,jsiqw->jaiqw", own_select, chosen, preferred_element_type=jnp.float32
    ).astype(jnp.bfloat16)
    received = lax.all_to_all(outgoing, "col", split_axis=0, concat_axis=0, tiled=True)
    held_rows = ancestor_rows.shape[0]
    received = received.reshape(col_devices, held_rows, slot_count, own_height, panel_count, width)
    all_targets = target_rows.reshape(col_devices, supernodes, panel_count)
    held_order = lax.dynamic_slice_in_dim(owner_order, col_place * held_rows, held_rows, 0)
    all_select = jax.vmap(lambda targets: slot_select(targets, held_order, slot_count))(all_targets)
    all_onehot = (all_targets[:, :, :, None] == block_ids).astype(jnp.float32)
    column_map = jnp.einsum("ckas,csqb->ckaqb", all_select, all_onehot).astype(jnp.bfloat16)
    spread = jnp.einsum(
        "ckaqb,ckaiqw->kibw", column_map, received, preferred_element_type=jnp.float32
    )
    summed = spread.reshape(held_rows, own_height, ancestors * width)
    return ancestor_rows - summed


PAIR = [(0, 1), (1, 0), (2, 3), (3, 2)]
MIDDLE = [(0, 0), (1, 2), (2, 1), (3, 3)]
CORE, X_HOP, Y_HOP = 1, 2, 4
OWN_ORDER = (0, Y_HOP, X_HOP, X_HOP | Y_HOP)
PAIR_ORDER = (0, X_HOP, Y_HOP, X_HOP | Y_HOP)


def row_swap(value, pairs):
    return lax.ppermute(value, "row", pairs)


def col_swap(value, mask):
    return lax.ppermute(value, "col", [(i, i ^ mask) for i in range(lax.axis_size("col"))])


def dot_t(a, b):
    return lax.dot_general(a, b, (((1,), (1,)), ((), ())), preferred_element_type=F32)


def solve_kernel(panel_ref, inverse_ref, out_ref):
    out_ref[...] = dot_t(panel_ref[...], inverse_ref[...]).astype(BF16)


def solve_part(panel, inverse, first, count, tile):
    width = panel.shape[1]
    base = first // tile
    return pl.pallas_call(
        solve_kernel,
        grid=(count // tile,),
        in_specs=[
            pl.BlockSpec((tile, width), lambda i: (base + i, 0)),
            pl.BlockSpec((width, width), lambda i: (0, 0)),
        ],
        out_specs=pl.BlockSpec((tile, width), lambda i: (i, 0)),
        out_shape=jax.ShapeDtypeStruct((count, width), BF16),
        cost_estimate=pl.CostEstimate(
            flops=2 * count * width * width, bytes_accessed=4 * count * width + 2 * width * width, transcendentals=0
        ),
        compiler_params=pltpu.CompilerParams(vmem_limit_bytes=VMEM_LIMIT),
        name="solve_part",
    )(panel, inverse)


def pick_kernel(height, order_ref, own0, own1, ownb0, ownb1, pair0, pair1, pairb0, pairb1, out_ref):
    col = lax.axis_index("col")
    half = own0.shape[0]
    width = own0.shape[1]

    def put(place, mask, parts):
        start = order_ref[jnp.bitwise_xor(col, mask)] * height
        for number, (low, high) in enumerate(parts):
            rows = pl.ds(place * height, height)
            columns = pl.ds(number * width, width)

            @pl.when(start < half)
            def _():
                out_ref[rows, columns] = low[pl.ds(pl.multiple_of(start, height), height), :]

            @pl.when(start >= half)
            def _():
                out_ref[rows, columns] = high[pl.ds(pl.multiple_of(start - half, height), height), :]

    for place, mask in enumerate(OWN_ORDER):
        put(place, mask, ((own0, own1), (ownb0, ownb1)))
    for place, mask in enumerate(PAIR_ORDER):
        put(len(OWN_ORDER) + place, mask, ((pair0, pair1), (pairb0, pairb1)))


def pick_blocks(order, height, arrays):
    half, width = arrays[0].shape
    rows = 2 * len(OWN_ORDER) * height
    whole = pl.BlockSpec(memory_space=pltpu.VMEM)
    return pl.pallas_call(
        functools.partial(pick_kernel, height),
        in_specs=[pl.BlockSpec(memory_space=pltpu.SMEM)] + [whole] * len(arrays),
        out_specs=whole,
        out_shape=jax.ShapeDtypeStruct((rows, 2 * width), BF16),
        cost_estimate=pl.CostEstimate(flops=0, bytes_accessed=2 * len(arrays) * half * width + 4 * rows * width, transcendentals=0),
        compiler_params=pltpu.CompilerParams(vmem_limit_bytes=VMEM_LIMIT),
        name="pick_blocks",
    )(order, *arrays)


def product_kernel(a_ref, xa_ref, xb_ref, own_keep, own_send, pair_keep, pair_send):
    width = xa_ref.shape[1]
    result = dot_t(a_ref[:, :width], xa_ref[...]) + dot_t(a_ref[:, width:], xb_ref[...])
    for step, out in enumerate((own_keep, own_send, pair_keep, pair_send)):

        @pl.when(pl.program_id(0) == step)
        def _():
            out[...] = result.astype(out.dtype)


def products(a, xa, xb):
    rows, depth = a.shape
    tile = rows // 4
    count, width = xa.shape
    fixed = lambda i: (0, 0)
    shapes = [jax.ShapeDtypeStruct((tile, count), t) for t in (F32, BF16, F32, BF16)]
    return pl.pallas_call(
        product_kernel,
        grid=(4,),
        in_specs=[
            pl.BlockSpec((tile, depth), lambda i: (i, 0)),
            pl.BlockSpec((count, width), fixed),
            pl.BlockSpec((count, width), fixed),
        ],
        out_specs=[pl.BlockSpec((tile, count), fixed)] * 4,
        out_shape=shapes,
        cost_estimate=pl.CostEstimate(
            flops=2 * rows * depth * count, bytes_accessed=2 * rows * depth + 4 * count * width + 3 * rows * count, transcendentals=0
        ),
        compiler_params=pltpu.CompilerParams(vmem_limit_bytes=VMEM_LIMIT),
        name="products",
    )(a, xa, xb)


def reduce_chunk(a, xa, xb, height):
    own_keep, own_send, pair_keep, pair_send = products(a, xa, xb)
    own_got = col_swap(own_send, X_HOP).astype(F32)
    pair_got = col_swap(pair_send, Y_HOP).astype(F32)
    own_half = own_keep[:height] + own_got[:height]
    own_next = (own_keep[height:] + own_got[height:]).astype(BF16)
    pair_half = pair_keep[:height] + pair_got[:height]
    pair_next = (pair_keep[height:] + pair_got[height:]).astype(BF16)
    own_last = col_swap(own_next, Y_HOP)
    pair_last = col_swap(pair_next, X_HOP)
    pair_done = (pair_half + pair_last.astype(F32)).astype(BF16)
    return own_half, own_last, row_swap(pair_done, PAIR)


def finish_kernel(height, places, anc_ref, *refs):
    out_ref = refs[-1]
    parts = refs[:-1]
    row = lax.axis_index("row")
    width = 4 * height
    low = row & 1
    high = row >> 1
    own_first = jnp.bitwise_or(low * 2, high)
    spots = (own_first, jnp.bitwise_xor(own_first, 1), jnp.bitwise_xor(own_first, 2), jnp.bitwise_xor(own_first, 3))
    for number, (which, first, count) in enumerate(places):
        half, last, back = parts[3 * number : 3 * number + 3]
        for block in range(count):
            source = pl.ds(block * height, height)
            own_at = pl.ds(pl.multiple_of((first + block) * width + spots[which] * height, height), height)
            pair_at = pl.ds(pl.multiple_of((first + block) * width + spots[2 + which] * height, height), height)
            out_ref[:, own_at] = anc_ref[:, own_at] - (half[:, source] + last[:, source].astype(F32))
            out_ref[:, pair_at] = anc_ref[:, pair_at] - back[:, source].astype(F32)


def finish(ancestor, places, parts, height):
    whole = pl.BlockSpec(memory_space=pltpu.VMEM)
    return pl.pallas_call(
        functools.partial(finish_kernel, height, places),
        in_specs=[whole] * (1 + len(parts)),
        out_specs=whole,
        out_shape=jax.ShapeDtypeStruct(ancestor.shape, F32),
        cost_estimate=pl.CostEstimate(flops=2 * ancestor.size, bytes_accessed=12 * ancestor.size, transcendentals=0),
        compiler_params=pltpu.CompilerParams(vmem_limit_bytes=VMEM_LIMIT),
        name="finish",
    )(ancestor, *parts)


def paired_body(panel_blocks, factor_inverse, target_rows, owner_order, ancestor_rows):
    _, panel_count, height, width = panel_blocks.shape
    panel = panel_blocks.reshape(panel_count * height, width)
    inverse = factor_inverse[0]
    half_blocks = panel_count // 2
    half = half_blocks * height
    own = [solve_part(panel, inverse, k * half, half, half // 2) for k in range(2)]
    first = [row_swap(s, MIDDLE) for s in own]
    pair = [row_swap(s, PAIR) for s in own]
    second = [row_swap(s, MIDDLE) for s in pair]
    own_b = [col_swap(s, CORE) for s in own]
    pair_b = [col_swap(s, CORE) for s in pair]
    a = pick_blocks(owner_order, height, [*own, *own_b, *pair, *pair_b])
    places = []
    parts = []
    for which, arrays in enumerate((first, second)):
        for k in range(2):
            parts += reduce_chunk(a, arrays[k], col_swap(arrays[k], CORE), height)
            places.append((which, k * half_blocks, half_blocks))
    result = finish(ancestor_rows[0], tuple(places), parts, height)
    return result[None]


def solution(mesh):
    def body(panel_blocks, factor_inverse, target_rows, owner_order, ancestor_rows):
        supernodes, panel_count, height, _ = panel_blocks.shape
        held = ancestor_rows.shape[0]
        paired = (
            mesh.shape["row"] == 4
            and mesh.shape["col"] == 8
            and panel_count == owner_order.shape[0] == 8
            and supernodes == 1
            and held == 1
            and height % 128 == 0
        )
        chosen = paired_body if paired else general_body
        return chosen(panel_blocks, factor_inverse, target_rows, owner_order, ancestor_rows)

    return jax.shard_map(
        body,
        mesh=mesh,
        in_specs=(
            P("col", None, "row", None),
            P("col", None, None),
            P(),
            P(),
            P("col", "row", None),
        ),
        out_specs=P("col", "row", None),
        check_vma=False,
    )
```

```python
import functools

import jax
import jax.numpy as jnp
from jax import lax
from jax.experimental import pallas as pl
from jax.experimental.pallas import tpu as pltpu
from jax.sharding import PartitionSpec as P

BF16 = jnp.bfloat16
F32 = jnp.float32
VMEM_LIMIT = 16 * 1024 * 1024
HINT = pl.CostEstimate(flops=1, bytes_accessed=1, transcendentals=0)


def solve_rows(blocks, factor_inverse):
    return jnp.einsum(
        "spiw,svw->spiv", blocks, factor_inverse, preferred_element_type=jnp.float32
    ).astype(jnp.bfloat16)


def pick_rows(products, own_targets, order_part):
    matched = own_targets[None, :, :] == order_part[:, None, None]
    places = lax.broadcasted_iota(jnp.int32, matched.shape, 2)
    position = jnp.sum(jnp.where(matched, places, 0), axis=2)
    present = jnp.any(matched, axis=2)
    supernode_ids = lax.broadcasted_iota(jnp.int32, position.shape, 1)
    chosen = products[supernode_ids, position]
    return jnp.where(present[:, :, None, None, None], chosen, jnp.zeros((), chosen.dtype))


def slot_select(targets, order_part, slot_count):
    matched = targets[None, :, :] == order_part[:, None, None]
    present = jnp.any(matched, axis=2)
    rank = jnp.cumsum(present.astype(jnp.int32), axis=1) - 1
    slot_ids = lax.broadcasted_iota(jnp.int32, (1, slot_count, 1), 1)
    selected = present[:, None, :] & (rank[:, None, :] == slot_ids)
    return selected.astype(jnp.float32)


def general_body(panel_blocks, factor_inverse, target_rows, owner_order, ancestor_rows):
    supernodes = panel_blocks.shape[0]
    panel_count = panel_blocks.shape[1]
    own_height = panel_blocks.shape[2]
    width = panel_blocks.shape[3]
    ancestors = owner_order.shape[0]
    col_devices = lax.axis_size("col")
    col_place = lax.axis_index("col")
    own_targets = lax.dynamic_slice_in_dim(target_rows, col_place * supernodes, supernodes, 0)
    own_solved = solve_rows(panel_blocks, factor_inverse)
    products = jnp.einsum(
        "spiw,sqmw->spiqm",
        own_solved,
        lax.all_gather(own_solved, "row", axis=2, tiled=True),
        preferred_element_type=jnp.float32,
    ).astype(jnp.bfloat16)
    block_ids = lax.broadcasted_iota(jnp.int32, (1, 1, 1, ancestors), 3)
    slot_count = (supernodes * panel_count + ancestors - 1) // ancestors
    chosen = pick_rows(products, own_targets, owner_order)
    own_select = slot_select(own_targets, owner_order, slot_count).astype(jnp.bfloat16)
    outgoing = jnp.einsum(
        "jas,jsiqw->jaiqw", own_select, chosen, preferred_element_type=jnp.float32
    ).astype(jnp.bfloat16)
    received = lax.all_to_all(outgoing, "col", split_axis=0, concat_axis=0, tiled=True)
    held_rows = ancestor_rows.shape[0]
    received = received.reshape(col_devices, held_rows, slot_count, own_height, panel_count, width)
    all_targets = target_rows.reshape(col_devices, supernodes, panel_count)
    held_order = lax.dynamic_slice_in_dim(owner_order, col_place * held_rows, held_rows, 0)
    all_select = jax.vmap(lambda targets: slot_select(targets, held_order, slot_count))(all_targets)
    all_onehot = (all_targets[:, :, :, None] == block_ids).astype(jnp.float32)
    column_map = jnp.einsum("ckas,csqb->ckaqb", all_select, all_onehot).astype(jnp.bfloat16)
    spread = jnp.einsum(
        "ckaqb,ckaiqw->kibw", column_map, received, preferred_element_type=jnp.float32
    )
    summed = spread.reshape(held_rows, own_height, ancestors * width)
    return ancestor_rows - summed


PAIR = (1, 0, 3, 2)
MIDDLE = (0, 2, 1, 3)
CORE, X_HOP, Y_HOP = 1, 2, 4
FIRST_HOP = (X_HOP, Y_HOP)
SECOND_HOP = (Y_HOP, X_HOP)


def row_swap(value, partner):
    return lax.ppermute(value, "row", list(enumerate(partner)))


def core_swap(value):
    return lax.ppermute(value, "col", [(i, i ^ CORE) for i in range(lax.axis_size("col"))])


def hop_swap(value, hops):
    return lax.ppermute(value, "col", [(i, i ^ hops[i & CORE]) for i in range(lax.axis_size("col"))])


def both_swap(value, partner, hops):
    cols = lax.axis_size("col")
    pairs = [(r * cols + c, partner[r] * cols + (c ^ hops[c & CORE])) for r in range(len(partner)) for c in range(cols)]
    return lax.ppermute(value, ("row", "col"), pairs)


def after(value, *others):
    return lax.optimization_barrier((value, *others))[0]


def dot_t(a, b):
    return lax.dot_general(a, b, (((1,), (1,)), ((), ())), preferred_element_type=F32)


def local_call(kernel, operands, shapes, name, scalars=0):
    whole = pl.BlockSpec(memory_space=pltpu.VMEM)
    return pl.pallas_call(
        kernel,
        in_specs=[pl.BlockSpec(memory_space=pltpu.SMEM)] * scalars + [whole] * (len(operands) - scalars),
        out_specs=[whole] * len(shapes),
        out_shape=[jax.ShapeDtypeStruct(shape, dtype) for shape, dtype in shapes],
        cost_estimate=HINT,
        compiler_params=pltpu.CompilerParams(vmem_limit_bytes=VMEM_LIMIT),
        name=name,
    )(*operands)


def core_index():
    return lax.axis_index("col") & CORE


def aligned(start, unit):
    return pl.ds(pl.multiple_of(start * unit, unit), unit)


def solve_kernel(panel_ref, inverse_ref, mine_ref, give_ref, rest_ref):
    half = give_ref.shape[0]
    for part in range(2):
        rows = pl.ds(part * half, half)
        solved = dot_t(panel_ref[rows, :], inverse_ref[...]).astype(BF16)
        mine_ref[rows, :] = solved

        @pl.when(core_index() != part)
        def _():
            give_ref[...] = solved

        @pl.when(core_index() == part)
        def _():
            rest_ref[...] = solved


def join_kernel(rest_ref, got_ref, *outs):
    width = rest_ref.shape[1]
    core = core_index()
    for out, first in zip(outs, (0, 0, outs[1].shape[0])):
        rows = pl.ds(first, out.shape[0])
        out[:, aligned(core, width)] = rest_ref[rows, :]
        out[:, aligned(1 - core, width)] = got_ref[rows, :]


def slot_masks():
    core = core_index()
    hop = jnp.where(core == 0, FIRST_HOP[0], FIRST_HOP[1])
    next_hop = jnp.where(core == 0, SECOND_HOP[0], SECOND_HOP[1])
    return [jnp.bitwise_xor(chip, side) for chip in (0, next_hop, hop, X_HOP | Y_HOP) for side in (0, CORE)]


def pick_own_kernel(height, order_ref, mine_ref, got_ref, got_rest_ref, out_ref):
    col, core = lax.axis_index("col"), core_index()
    half, width = got_ref.shape
    for place, mask in enumerate(slot_masks()):
        start = order_ref[jnp.bitwise_xor(col, mask)] * height
        rows = pl.ds(place * height, height)
        out_ref[rows, aligned(core, width)] = mine_ref[pl.ds(pl.multiple_of(start, height), height), :]
        inside = start // half == core
        source = pl.ds(pl.multiple_of(start % half, height), height)

        @pl.when(inside)
        def _():
            out_ref[rows, aligned(1 - core, width)] = got_ref[source, :]

        @pl.when(jnp.logical_not(inside))
        def _():
            out_ref[rows, aligned(1 - core, width)] = got_rest_ref[source, :]


def pick_pair_kernel(height, pieces, order_ref, *refs):
    out_ref = refs[-1]
    col, core = lax.axis_index("col"), core_index()
    half = sum(ref.shape[0] for ref in refs[:pieces])
    for place, mask in enumerate(slot_masks()):
        start = order_ref[jnp.bitwise_xor(col, mask)] * height
        rows = pl.ds(place * height, height)
        inside = start // half == core
        within = start % half
        for number in range(2 * pieces):
            ref = refs[number]
            first = sum(r.shape[0] for r in refs[: number % pieces])
            here = jnp.logical_and(within >= first, within < first + ref.shape[0])
            wanted = inside if number < pieces else jnp.logical_not(inside)

            @pl.when(jnp.logical_and(here, wanted))
            def _():
                out_ref[rows, :] = ref[pl.ds(pl.multiple_of(within - first, height), height), :]


def product_kernel(count, *refs):
    x_ref, keep_ref, send_ref = refs[count:]
    for number, a_ref in enumerate(refs[:count]):
        tile = a_ref.shape[0] // 2
        rows = pl.ds(number * tile, tile)
        keep_ref[rows, :] = dot_t(a_ref[:tile, :], x_ref[...])
        send_ref[rows, :] = dot_t(a_ref[tile:, :], x_ref[...]).astype(BF16)


def products(a, x):
    shape = (sum(part.shape[0] for part in a) // 2, x.shape[0])
    return local_call(functools.partial(product_kernel, len(a)), [*a, x], [(shape, F32), (shape, BF16)], "products")


def own_second(keep, got):
    total = keep + got.astype(F32)
    half = total.shape[0] // 2
    return total[:half], hop_swap(total[half:].astype(BF16), SECOND_HOP)


def pair_second(keep, got):
    total = (keep + got.astype(F32)).astype(BF16)
    half = total.shape[0] // 2
    return row_swap(total[:half], PAIR), both_swap(total[half:], PAIR, SECOND_HOP)


def pack(terms, height):
    return jnp.concatenate([term[height:].astype(BF16) for term in terms], axis=0)


def finish_kernel(height, plan, anc_ref, *refs):
    out_ref = refs[-1]
    row, core = lax.axis_index("row"), core_index()
    width = 4 * height
    half = out_ref.shape[1] // 2
    base = jnp.bitwise_or((row & 1) * 2, row >> 1)
    for number, (which, first, count) in enumerate(plan):
        *terms, other = refs[5 * number : 5 * number + 5]
        for back in range(2):
            at = jnp.bitwise_xor(base, which + 2 * back)
            for block in range(count):
                source = pl.ds(block * height, height)
                for side in range(2):
                    place = (core if side == 0 else 1 - core) * half + (first + block) * width + at * height
                    place = pl.ds(pl.multiple_of(place, height), height)
                    if side == 0:
                        low, high = (terms[2 * back + k][:height, source] for k in range(2))
                    else:
                        low, high = (other[pl.ds((2 * back + k) * height, height), source] for k in range(2))
                    out_ref[:, place] = anc_ref[:, place] - (low.astype(F32) + high.astype(F32))


def paired_body(panel_blocks, factor_inverse, target_rows, owner_order, ancestor_rows):
    _, panel_count, height, width = panel_blocks.shape
    rows = panel_count * height
    panel = panel_blocks.reshape(rows, width)
    half = rows // 2
    pieces = (half // 2, half // 2)

    mine, give, rest = local_call(
        solve_kernel, [panel, factor_inverse[0]], [((rows, width), BF16)] + [((half, width), BF16)] * 2, "solve"
    )
    got = core_swap(give)
    got_rest = core_swap(rest)
    joined, *parts = local_call(
        join_kernel, [rest, got], [((count, 2 * width), BF16) for count in (half, *pieces)], "join"
    )
    first = row_swap(joined, MIDDLE)
    pair = [row_swap(part, PAIR) for part in parts]
    (a_own,) = local_call(
        functools.partial(pick_own_kernel, height),
        [owner_order, mine, got, got_rest],
        [((rows, 2 * width), BF16)],
        "pick_own",
        scalars=1,
    )
    pair[0] = after(pair[0], a_own)
    second = [row_swap(part, MIDDLE) for part in pair]
    (a_pair,) = local_call(
        functools.partial(pick_pair_kernel, height, len(pair)),
        [owner_order, *pair, *[core_swap(part) for part in pair]],
        [((rows, 2 * width), BF16)],
        "pick_pair",
        scalars=1,
    )

    own1, send = products([a_own], first)
    own1_got = hop_swap(send, FIRST_HOP)
    pair1, send = products([after(a_pair, own1)], first)
    pair1_got = hop_swap(send, FIRST_HOP)
    own1_terms = own_second(own1, after(own1_got, pair1))
    keep2, send = products([a_own, a_pair], after(second[0], own1_terms[0]))
    got2 = hop_swap(send, FIRST_HOP)
    terms1 = (*own1_terms, *pair_second(pair1, after(pair1_got, keep2)))
    keep3, send = products([a_own, a_pair], after(second[1], terms1[2]))
    got3 = hop_swap(send, FIRST_HOP)
    packed1 = pack((terms1[0], after(terms1[1], keep3), *terms1[2:]), height)
    other1 = core_swap(packed1)
    got2 = after(got2, packed1)
    terms2 = (*own_second(keep2[:half], got2[:half]), *pair_second(keep2[half:], got2[half:]))
    packed2 = pack(terms2, height)
    other2 = core_swap(packed2)
    got3 = after(got3, packed2)
    terms3 = (*own_second(keep3[:half], got3[:half]), *pair_second(keep3[half:], got3[half:]))
    other3 = core_swap(pack(terms3, height))
    blocks = [count // height for count in pieces]
    plan = ((0, 0, half // height), (1, 0, blocks[0]), (1, blocks[0], blocks[1]))
    (result,) = local_call(
        functools.partial(finish_kernel, height, plan),
        [ancestor_rows[0], *terms1, other1, *terms2, other2, *terms3, other3],
        [(ancestor_rows.shape[1:], F32)],
        "finish",
    )
    return result[None]


def solution(mesh):
    def body(panel_blocks, factor_inverse, target_rows, owner_order, ancestor_rows):
        supernodes, panel_count, height, _ = panel_blocks.shape
        held = ancestor_rows.shape[0]
        paired = (
            mesh.shape["row"] == 4
            and mesh.shape["col"] == 8
            and panel_count == owner_order.shape[0] == 8
            and supernodes == 1
            and held == 1
            and height % 128 == 0
        )
        chosen = paired_body if paired else general_body
        return chosen(panel_blocks, factor_inverse, target_rows, owner_order, ancestor_rows)

    return jax.shard_map(
        body,
        mesh=mesh,
        in_specs=(
            P("col", None, "row", None),
            P("col", None, None),
            P(),
            P(),
            P("col", "row", None),
        ),
        out_specs=P("col", "row", None),
        check_vma=False,
    )
```

```python
import functools

import jax
import jax.numpy as jnp
from jax import lax
from jax.experimental import pallas as pl
from jax.experimental.pallas import tpu as pltpu
from jax.sharding import PartitionSpec as P

BF16 = jnp.bfloat16
F32 = jnp.float32
VMEM_LIMIT = 16 * 1024 * 1024
HINT = pl.CostEstimate(flops=1, bytes_accessed=1, transcendentals=0)


def solve_rows(blocks, factor_inverse):
    return jnp.einsum(
        "spiw,svw->spiv", blocks, factor_inverse, preferred_element_type=jnp.float32
    ).astype(jnp.bfloat16)


def pick_rows(products, own_targets, order_part):
    matched = own_targets[None, :, :] == order_part[:, None, None]
    places = lax.broadcasted_iota(jnp.int32, matched.shape, 2)
    position = jnp.sum(jnp.where(matched, places, 0), axis=2)
    present = jnp.any(matched, axis=2)
    supernode_ids = lax.broadcasted_iota(jnp.int32, position.shape, 1)
    chosen = products[supernode_ids, position]
    return jnp.where(present[:, :, None, None, None], chosen, jnp.zeros((), chosen.dtype))


def slot_select(targets, order_part, slot_count):
    matched = targets[None, :, :] == order_part[:, None, None]
    present = jnp.any(matched, axis=2)
    rank = jnp.cumsum(present.astype(jnp.int32), axis=1) - 1
    slot_ids = lax.broadcasted_iota(jnp.int32, (1, slot_count, 1), 1)
    selected = present[:, None, :] & (rank[:, None, :] == slot_ids)
    return selected.astype(jnp.float32)


def general_body(panel_blocks, factor_inverse, target_rows, owner_order, ancestor_rows):
    supernodes = panel_blocks.shape[0]
    panel_count = panel_blocks.shape[1]
    own_height = panel_blocks.shape[2]
    width = panel_blocks.shape[3]
    ancestors = owner_order.shape[0]
    col_devices = lax.axis_size("col")
    col_place = lax.axis_index("col")
    own_targets = lax.dynamic_slice_in_dim(target_rows, col_place * supernodes, supernodes, 0)
    own_solved = solve_rows(panel_blocks, factor_inverse)
    products = jnp.einsum(
        "spiw,sqmw->spiqm",
        own_solved,
        lax.all_gather(own_solved, "row", axis=2, tiled=True),
        preferred_element_type=jnp.float32,
    ).astype(jnp.bfloat16)
    block_ids = lax.broadcasted_iota(jnp.int32, (1, 1, 1, ancestors), 3)
    slot_count = (supernodes * panel_count + ancestors - 1) // ancestors
    chosen = pick_rows(products, own_targets, owner_order)
    own_select = slot_select(own_targets, owner_order, slot_count).astype(jnp.bfloat16)
    outgoing = jnp.einsum(
        "jas,jsiqw->jaiqw", own_select, chosen, preferred_element_type=jnp.float32
    ).astype(jnp.bfloat16)
    received = lax.all_to_all(outgoing, "col", split_axis=0, concat_axis=0, tiled=True)
    held_rows = ancestor_rows.shape[0]
    received = received.reshape(col_devices, held_rows, slot_count, own_height, panel_count, width)
    all_targets = target_rows.reshape(col_devices, supernodes, panel_count)
    held_order = lax.dynamic_slice_in_dim(owner_order, col_place * held_rows, held_rows, 0)
    all_select = jax.vmap(lambda targets: slot_select(targets, held_order, slot_count))(all_targets)
    all_onehot = (all_targets[:, :, :, None] == block_ids).astype(jnp.float32)
    column_map = jnp.einsum("ckas,csqb->ckaqb", all_select, all_onehot).astype(jnp.bfloat16)
    spread = jnp.einsum(
        "ckaqb,ckaiqw->kibw", column_map, received, preferred_element_type=jnp.float32
    )
    summed = spread.reshape(held_rows, own_height, ancestors * width)
    return ancestor_rows - summed


PAIR = (1, 0, 3, 2)
MIDDLE = (0, 2, 1, 3)
CORE, X_HOP, Y_HOP = 1, 2, 4
FIRST_HOP = (X_HOP, Y_HOP)
SECOND_HOP = (Y_HOP, X_HOP)


def row_swap(value, partner):
    return lax.ppermute(value, "row", list(enumerate(partner)))


def core_swap(value):
    return lax.ppermute(value, "col", [(i, i ^ CORE) for i in range(lax.axis_size("col"))])


def hop_swap(value, hops):
    return lax.ppermute(value, "col", [(i, i ^ hops[i & CORE]) for i in range(lax.axis_size("col"))])


def both_swap(value, partner, hops):
    cols = lax.axis_size("col")
    pairs = [(r * cols + c, partner[r] * cols + (c ^ hops[c & CORE])) for r in range(len(partner)) for c in range(cols)]
    return lax.ppermute(value, ("row", "col"), pairs)


def after(value, *others):
    return lax.optimization_barrier((value, *others))[0]


def dot_t(a, b):
    return lax.dot_general(a, b, (((1,), (1,)), ((), ())), preferred_element_type=F32)


def local_call(kernel, operands, shapes, name, scalars=0):
    whole = pl.BlockSpec(memory_space=pltpu.VMEM)
    return pl.pallas_call(
        kernel,
        in_specs=[pl.BlockSpec(memory_space=pltpu.SMEM)] * scalars + [whole] * (len(operands) - scalars),
        out_specs=[whole] * len(shapes),
        out_shape=[jax.ShapeDtypeStruct(shape, dtype) for shape, dtype in shapes],
        cost_estimate=HINT,
        compiler_params=pltpu.CompilerParams(vmem_limit_bytes=VMEM_LIMIT),
        name=name,
    )(*operands)


def core_index():
    return lax.axis_index("col") & CORE


def aligned(start, unit):
    return pl.ds(pl.multiple_of(start * unit, unit), unit)


def solve_kernel(other, panel_ref, inverse_ref, out_ref):
    part = 1 - core_index() if other else core_index()
    rows = aligned(part, out_ref.shape[0])
    out_ref[...] = dot_t(panel_ref[rows, :], inverse_ref[...]).astype(BF16)


def join_kernel(rest_ref, got_ref, *outs):
    width = rest_ref.shape[1]
    core = core_index()
    half = outs[0].shape[0]
    for out, first in zip(outs, (0, 0, half - outs[2].shape[0])):
        rows = pl.ds(first, out.shape[0])
        out[:, aligned(core, width)] = rest_ref[rows, :]
        out[:, aligned(1 - core, width)] = got_ref[rows, :]


def slot_masks():
    core = core_index()
    hop = jnp.where(core == 0, FIRST_HOP[0], FIRST_HOP[1])
    next_hop = jnp.where(core == 0, SECOND_HOP[0], SECOND_HOP[1])
    return [jnp.bitwise_xor(chip, side) for chip in (0, next_hop, hop, X_HOP | Y_HOP) for side in (0, CORE)]


def pick_own_kernel(height, order_ref, rest_ref, give_ref, got_ref, got_rest_ref, out_ref):
    col, core = lax.axis_index("col"), core_index()
    half, width = rest_ref.shape
    for place, mask in enumerate(slot_masks()):
        start = order_ref[jnp.bitwise_xor(col, mask)] * height
        rows = pl.ds(place * height, height)
        inside = start // half == core
        source = pl.ds(pl.multiple_of(start % half, height), height)
        for wanted, mine, other in ((inside, rest_ref, got_ref), (jnp.logical_not(inside), give_ref, got_rest_ref)):

            @pl.when(wanted)
            def _():
                out_ref[rows, aligned(core, width)] = mine[source, :]
                out_ref[rows, aligned(1 - core, width)] = other[source, :]


def pick_pair_kernel(height, valid, order_ref, *refs):
    pieces = len(valid)
    out_ref = refs[-1]
    col, core = lax.axis_index("col"), core_index()
    half = sum(count for _, count in valid)
    for place, mask in enumerate(slot_masks()):
        start = order_ref[jnp.bitwise_xor(col, mask)] * height
        rows = pl.ds(place * height, height)
        inside = start // half == core
        within = start % half
        for number in range(2 * pieces):
            ref = refs[number]
            skip, count = valid[number % pieces]
            first = sum(c for _, c in valid[: number % pieces])
            here = jnp.logical_and(within >= first, within < first + count)
            first = first - skip
            wanted = inside if number < pieces else jnp.logical_not(inside)

            @pl.when(jnp.logical_and(here, wanted))
            def _():
                out_ref[rows, :] = ref[pl.ds(pl.multiple_of(within - first, height), height), :]


def product_kernel(count, *refs):
    x_ref, keep_ref, send_ref = refs[count:]
    for number, a_ref in enumerate(refs[:count]):
        tile = a_ref.shape[0] // 2
        rows = pl.ds(number * tile, tile)
        keep_ref[rows, :] = dot_t(a_ref[:tile, :], x_ref[...])
        send_ref[rows, :] = dot_t(a_ref[tile:, :], x_ref[...]).astype(BF16)


def products(a, x):
    shape = (sum(part.shape[0] for part in a) // 2, x.shape[0])
    return local_call(functools.partial(product_kernel, len(a)), [*a, x], [(shape, F32), (shape, BF16)], "products")


def own_ways(total):
    half = total.shape[0] // 2
    return total[:half], hop_swap(total[half:].astype(BF16), SECOND_HOP)


def pair_ways(total):
    half = total.shape[0] // 2
    total = total.astype(BF16)
    return row_swap(total[:half], PAIR), both_swap(total[half:], PAIR, SECOND_HOP), total


def pack(terms, height):
    return jnp.concatenate([term[height : 2 * height].astype(BF16) for term in terms], axis=0)


def finish_kernel(height, plan, anc_ref, *refs):
    out_ref = refs[-1]
    row, core = lax.axis_index("row"), core_index()
    width = 4 * height
    half = out_ref.shape[1] // 2
    base = jnp.bitwise_or((row & 1) * 2, row >> 1)
    position = 0
    for which, first, count, terms in plan:
        mine = refs[position : position + terms]
        other = refs[position + terms]
        position += terms + 1
        for returned, wanted in enumerate((range(2), range(2, terms))):
            at = jnp.bitwise_xor(base, which + 2 * returned)
            for block in range(count):
                source = pl.ds(block * height, height)
                for side in range(2):
                    tiles = [other[pl.ds(k * height, height), source] if side else mine[k][:height, source] for k in wanted]
                    total = sum(tile.astype(F32) for tile in tiles)
                    place = (1 - core if side else core) * half + (first + block) * width + at * height
                    place = pl.ds(pl.multiple_of(place, height), height)
                    out_ref[:, place] = anc_ref[:, place] - total


def paired_body(panel_blocks, factor_inverse, target_rows, owner_order, ancestor_rows):
    _, panel_count, height, width = panel_blocks.shape
    rows = panel_count * height
    panel = panel_blocks.reshape(rows, width)
    half = rows // 2
    pieces = (2 * height, half - 2 * height)
    valid = [(0, count) for count in pieces]

    inverse = factor_inverse[0]
    half_shape = [((half, width), BF16)]
    (give,) = local_call(functools.partial(solve_kernel, True), [panel, inverse], half_shape, "solve")
    got = core_swap(give)
    (rest,) = local_call(functools.partial(solve_kernel, False), [panel, after(inverse, give)], half_shape, "solve")
    got_rest = core_swap(rest)
    joined, *parts = local_call(
        join_kernel, [rest, got], [((count, 2 * width), BF16) for count in (half, *pieces)], "join"
    )
    pair = [row_swap(part, PAIR) for part in parts]
    (a_own,) = local_call(
        functools.partial(pick_own_kernel, height),
        [owner_order, rest, give, got, got_rest],
        [((rows, 2 * width), BF16)],
        "pick_own",
        scalars=1,
    )
    first = row_swap(after(joined, a_own), MIDDLE)
    second = [row_swap(after(pair[0], a_own), MIDDLE), row_swap(pair[1], MIDDLE)]
    pair_b = core_swap(pair[0])
    (a_pair,) = local_call(
        functools.partial(pick_pair_kernel, height, valid),
        [owner_order, *pair, pair_b, core_swap(after(pair[1], pair_b))],
        [((rows, 2 * width), BF16)],
        "pick_pair",
        scalars=1,
    )
    keep_own, send = products([a_own], first)
    got_own = hop_swap(send, FIRST_HOP)
    keep_pair, send = products([after(a_pair, keep_own)], first)
    got_pair = hop_swap(send, FIRST_HOP)
    keep2, send = products([a_own, a_pair], after(second[0], keep_pair))
    got2 = hop_swap(send, FIRST_HOP)
    own1 = own_ways(keep_own + after(got_own, keep2).astype(F32))
    *pair1, sent1 = pair_ways(keep_pair + after(got_pair, own1[0]).astype(F32))
    keep3, send = products([a_own, a_pair], after(second[1], sent1))
    got3 = hop_swap(send, FIRST_HOP)
    terms1 = (*own1, pair1[0], after(pair1[1], keep3))
    packed1 = pack(terms1, height)
    other1 = core_swap(packed1)
    total2 = keep2 + after(got2, packed1).astype(F32)
    own2 = own_ways(total2[:half])
    *pair2, sent2 = pair_ways(total2[half:])
    terms2 = (*own2, pair2[0], after(pair2[1], sent2))
    packed2 = pack(terms2, height)
    other2 = core_swap(packed2)
    total3 = keep3 + after(got3, packed2).astype(F32)
    own3 = own_ways(total3[:half])
    *pair3, sent3 = pair_ways(total3[half:])
    terms3 = (*own3, pair3[0], after(pair3[1], sent3))
    packed3 = pack(terms3, height)
    other3 = core_swap(packed3)
    blocks = [count // height for count in pieces]
    plan = ((0, 0, half // height, len(terms1)), (1, 0, blocks[0], len(terms2)), (1, blocks[0], blocks[1], len(terms3)))
    (result,) = local_call(
        functools.partial(finish_kernel, height, plan),
        [ancestor_rows[0], *terms1, other1, *terms2, other2, *terms3, other3],
        [(ancestor_rows.shape[1:], F32)],
        "finish",
    )
    return result[None]


def solution(mesh):
    def body(panel_blocks, factor_inverse, target_rows, owner_order, ancestor_rows):
        supernodes, panel_count, height, _ = panel_blocks.shape
        held = ancestor_rows.shape[0]
        paired = (
            mesh.shape["row"] == 4
            and mesh.shape["col"] == 8
            and panel_count == owner_order.shape[0] == 8
            and supernodes == 1
            and held == 1
            and height % 128 == 0
        )
        chosen = paired_body if paired else general_body
        return chosen(panel_blocks, factor_inverse, target_rows, owner_order, ancestor_rows)

    return jax.shard_map(
        body,
        mesh=mesh,
        in_specs=(
            P("col", None, "row", None),
            P("col", None, None),
            P(),
            P(),
            P("col", "row", None),
        ),
        out_specs=P("col", "row", None),
        check_vma=False,
    )
```

```python
import functools

import jax
import jax.numpy as jnp
from jax import lax
from jax.experimental import pallas as pl
from jax.experimental.pallas import tpu as pltpu
from jax.sharding import PartitionSpec as P

BF16 = jnp.bfloat16
F32 = jnp.float32
VMEM_LIMIT = 16 * 1024 * 1024
HINT = pl.CostEstimate(flops=1, bytes_accessed=1, transcendentals=0)


def solve_rows(blocks, factor_inverse):
    return jnp.einsum(
        "spiw,svw->spiv", blocks, factor_inverse, preferred_element_type=jnp.float32
    ).astype(jnp.bfloat16)


def pick_rows(products, own_targets, order_part):
    matched = own_targets[None, :, :] == order_part[:, None, None]
    places = lax.broadcasted_iota(jnp.int32, matched.shape, 2)
    position = jnp.sum(jnp.where(matched, places, 0), axis=2)
    present = jnp.any(matched, axis=2)
    supernode_ids = lax.broadcasted_iota(jnp.int32, position.shape, 1)
    chosen = products[supernode_ids, position]
    return jnp.where(present[:, :, None, None, None], chosen, jnp.zeros((), chosen.dtype))


def slot_select(targets, order_part, slot_count):
    matched = targets[None, :, :] == order_part[:, None, None]
    present = jnp.any(matched, axis=2)
    rank = jnp.cumsum(present.astype(jnp.int32), axis=1) - 1
    slot_ids = lax.broadcasted_iota(jnp.int32, (1, slot_count, 1), 1)
    selected = present[:, None, :] & (rank[:, None, :] == slot_ids)
    return selected.astype(jnp.float32)


def general_body(panel_blocks, factor_inverse, target_rows, owner_order, ancestor_rows):
    supernodes = panel_blocks.shape[0]
    panel_count = panel_blocks.shape[1]
    own_height = panel_blocks.shape[2]
    width = panel_blocks.shape[3]
    ancestors = owner_order.shape[0]
    col_devices = lax.axis_size("col")
    col_place = lax.axis_index("col")
    own_targets = lax.dynamic_slice_in_dim(target_rows, col_place * supernodes, supernodes, 0)
    own_solved = solve_rows(panel_blocks, factor_inverse)
    products = jnp.einsum(
        "spiw,sqmw->spiqm",
        own_solved,
        lax.all_gather(own_solved, "row", axis=2, tiled=True),
        preferred_element_type=jnp.float32,
    ).astype(jnp.bfloat16)
    block_ids = lax.broadcasted_iota(jnp.int32, (1, 1, 1, ancestors), 3)
    slot_count = (supernodes * panel_count + ancestors - 1) // ancestors
    chosen = pick_rows(products, own_targets, owner_order)
    own_select = slot_select(own_targets, owner_order, slot_count).astype(jnp.bfloat16)
    outgoing = jnp.einsum(
        "jas,jsiqw->jaiqw", own_select, chosen, preferred_element_type=jnp.float32
    ).astype(jnp.bfloat16)
    received = lax.all_to_all(outgoing, "col", split_axis=0, concat_axis=0, tiled=True)
    held_rows = ancestor_rows.shape[0]
    received = received.reshape(col_devices, held_rows, slot_count, own_height, panel_count, width)
    all_targets = target_rows.reshape(col_devices, supernodes, panel_count)
    held_order = lax.dynamic_slice_in_dim(owner_order, col_place * held_rows, held_rows, 0)
    all_select = jax.vmap(lambda targets: slot_select(targets, held_order, slot_count))(all_targets)
    all_onehot = (all_targets[:, :, :, None] == block_ids).astype(jnp.float32)
    column_map = jnp.einsum("ckas,csqb->ckaqb", all_select, all_onehot).astype(jnp.bfloat16)
    spread = jnp.einsum(
        "ckaqb,ckaiqw->kibw", column_map, received, preferred_element_type=jnp.float32
    )
    summed = spread.reshape(held_rows, own_height, ancestors * width)
    return ancestor_rows - summed


PAIR = (1, 0, 3, 2)
MIDDLE = (0, 2, 1, 3)
CORE, X_HOP, Y_HOP = 1, 2, 4
FIRST_HOP = (X_HOP, Y_HOP)
SECOND_HOP = (Y_HOP, X_HOP)


def row_swap(value, partner):
    return lax.ppermute(value, "row", list(enumerate(partner)))


def core_swap(value):
    return lax.ppermute(value, "col", [(i, i ^ CORE) for i in range(lax.axis_size("col"))])


def hop_swap(value, hops):
    return lax.ppermute(value, "col", [(i, i ^ hops[i & CORE]) for i in range(lax.axis_size("col"))])


def both_swap(value, partner, hops):
    cols = lax.axis_size("col")
    pairs = [(r * cols + c, partner[r] * cols + (c ^ hops[c & CORE])) for r in range(len(partner)) for c in range(cols)]
    return lax.ppermute(value, ("row", "col"), pairs)


def after(value, *others):
    return lax.optimization_barrier((value, *others))[0]


def dot_t(a, b):
    return lax.dot_general(a, b, (((1,), (1,)), ((), ())), preferred_element_type=F32)


def local_call(kernel, operands, shapes, name, scalars=0):
    whole = pl.BlockSpec(memory_space=pltpu.VMEM)
    return pl.pallas_call(
        kernel,
        in_specs=[pl.BlockSpec(memory_space=pltpu.SMEM)] * scalars + [whole] * (len(operands) - scalars),
        out_specs=[whole] * len(shapes),
        out_shape=[jax.ShapeDtypeStruct(shape, dtype) for shape, dtype in shapes],
        cost_estimate=HINT,
        compiler_params=pltpu.CompilerParams(vmem_limit_bytes=VMEM_LIMIT),
        name=name,
    )(*operands)


def core_index():
    return lax.axis_index("col") & CORE


def aligned(start, unit):
    return pl.ds(pl.multiple_of(start * unit, unit), unit)


def solve_kernel(other, panel_ref, inverse_ref, out_ref):
    part = 1 - core_index() if other else core_index()
    rows = aligned(part, out_ref.shape[0])
    out_ref[...] = dot_t(panel_ref[rows, :], inverse_ref[...]).astype(BF16)


def join_kernel(rest_ref, got_ref, *outs):
    width = rest_ref.shape[1]
    core = core_index()
    half = outs[0].shape[0]
    for out, first in zip(outs, (0, 0, half - outs[2].shape[0])):
        rows = pl.ds(first, out.shape[0])
        out[:, aligned(core, width)] = rest_ref[rows, :]
        out[:, aligned(1 - core, width)] = got_ref[rows, :]


def slot_masks():
    core = core_index()
    hop = jnp.where(core == 0, FIRST_HOP[0], FIRST_HOP[1])
    next_hop = jnp.where(core == 0, SECOND_HOP[0], SECOND_HOP[1])
    return [jnp.bitwise_xor(chip, side) for chip in (0, next_hop, hop, X_HOP | Y_HOP) for side in (0, CORE)]


def pick_own_kernel(height, order_ref, rest_ref, give_ref, got_ref, got_rest_ref, out_ref):
    col, core = lax.axis_index("col"), core_index()
    half, width = rest_ref.shape
    for place, mask in enumerate(slot_masks()):
        start = order_ref[jnp.bitwise_xor(col, mask)] * height
        rows = pl.ds(place * height, height)
        inside = start // half == core
        source = pl.ds(pl.multiple_of(start % half, height), height)
        for wanted, mine, other in ((inside, rest_ref, got_ref), (jnp.logical_not(inside), give_ref, got_rest_ref)):

            @pl.when(wanted)
            def _():
                out_ref[rows, aligned(core, width)] = mine[source, :]
                out_ref[rows, aligned(1 - core, width)] = other[source, :]


def pick_pair_kernel(height, valid, order_ref, *refs):
    pieces = len(valid)
    out_ref = refs[-1]
    col, core = lax.axis_index("col"), core_index()
    half = sum(count for _, count in valid)
    for place, mask in enumerate(slot_masks()):
        start = order_ref[jnp.bitwise_xor(col, mask)] * height
        rows = pl.ds(place * height, height)
        inside = start // half == core
        within = start % half
        for number in range(2 * pieces):
            ref = refs[number]
            skip, count = valid[number % pieces]
            first = sum(c for _, c in valid[: number % pieces])
            here = jnp.logical_and(within >= first, within < first + count)
            first = first - skip
            wanted = inside if number < pieces else jnp.logical_not(inside)

            @pl.when(jnp.logical_and(here, wanted))
            def _():
                out_ref[rows, :] = ref[pl.ds(pl.multiple_of(within - first, height), height), :]


def product_kernel(count, *refs):
    x_ref, keep_ref, send_ref = refs[count:]
    for number, a_ref in enumerate(refs[:count]):
        tile = a_ref.shape[0] // 2
        rows = pl.ds(number * tile, tile)
        keep_ref[rows, :] = dot_t(a_ref[:tile, :], x_ref[...])
        send_ref[rows, :] = dot_t(a_ref[tile:, :], x_ref[...]).astype(BF16)


def products(a, x):
    shape = (sum(part.shape[0] for part in a) // 2, x.shape[0])
    return local_call(functools.partial(product_kernel, len(a)), [*a, x], [(shape, F32), (shape, BF16)], "products")


def own_ways(total):
    half = total.shape[0] // 2
    return total[:half], hop_swap(total[half:].astype(BF16), SECOND_HOP)


def pair_ways(total):
    half = total.shape[0] // 2
    total = total.astype(BF16)
    return row_swap(total[:half], PAIR), both_swap(total[half:], PAIR, SECOND_HOP), total


def pack(terms, height):
    return jnp.concatenate([term[height : 2 * height].astype(BF16) for term in terms], axis=0)


def finish_kernel(height, plan, anc_ref, *refs):
    out_ref = refs[-1]
    row, core = lax.axis_index("row"), core_index()
    width = 4 * height
    half = out_ref.shape[1] // 2
    base = jnp.bitwise_or((row & 1) * 2, row >> 1)
    position = 0
    for which, first, count, terms in plan:
        mine = refs[position : position + terms]
        other = refs[position + terms]
        position += terms + 1
        for returned, wanted in enumerate((range(2), range(2, terms))):
            at = jnp.bitwise_xor(base, which + 2 * returned)
            for block in range(count):
                source = pl.ds(block * height, height)
                for side in range(2):
                    tiles = [other[pl.ds(k * height, height), source] if side else mine[k][:height, source] for k in wanted]
                    total = sum(tile.astype(F32) for tile in tiles)
                    place = (1 - core if side else core) * half + (first + block) * width + at * height
                    place = pl.ds(pl.multiple_of(place, height), height)
                    out_ref[:, place] = anc_ref[:, place] - total


def paired_body(panel_blocks, factor_inverse, target_rows, owner_order, ancestor_rows):
    _, panel_count, height, width = panel_blocks.shape
    rows = panel_count * height
    panel = panel_blocks.reshape(rows, width)
    half = rows // 2
    pieces = (2 * height, half - 2 * height)
    valid = [(0, count) for count in pieces]

    inverse = factor_inverse[0]
    half_shape = [((half, width), BF16)]
    (give,) = local_call(functools.partial(solve_kernel, True), [panel, inverse], half_shape, "solve")
    got = core_swap(give)
    (rest,) = local_call(functools.partial(solve_kernel, False), [panel, after(inverse, give)], half_shape, "solve")
    got_rest = core_swap(rest)
    joined, *parts = local_call(
        join_kernel, [rest, got], [((count, 2 * width), BF16) for count in (half, *pieces)], "join"
    )
    pair = [row_swap(part, PAIR) for part in parts]
    (a_own,) = local_call(
        functools.partial(pick_own_kernel, height),
        [owner_order, rest, give, got, got_rest],
        [((rows, 2 * width), BF16)],
        "pick_own",
        scalars=1,
    )
    first = row_swap(after(joined, a_own), MIDDLE)
    second = [row_swap(after(pair[0], a_own), MIDDLE), row_swap(pair[1], MIDDLE)]
    pair_b = core_swap(pair[0])
    (a_pair,) = local_call(
        functools.partial(pick_pair_kernel, height, valid),
        [owner_order, *pair, pair_b, core_swap(after(pair[1], pair_b))],
        [((rows, 2 * width), BF16)],
        "pick_pair",
        scalars=1,
    )
    keep_own, send = products([a_own], first)
    got_own = hop_swap(send, FIRST_HOP)
    keep_pair, send = products([after(a_pair, keep_own)], first)
    got_pair = hop_swap(send, FIRST_HOP)
    keep2, send = products([a_own, a_pair], after(second[0], keep_pair))
    got2 = hop_swap(send, FIRST_HOP)
    own1 = own_ways(keep_own + after(got_own, keep2).astype(F32))
    *pair1, sent1 = pair_ways(keep_pair + after(got_pair, own1[0]).astype(F32))
    keep3, send = products([a_own, a_pair], after(second[1], keep2))
    got3 = hop_swap(send, FIRST_HOP)
    terms1 = (*own1, pair1[0], after(pair1[1], keep3))
    packed1 = pack(terms1, height)
    other1 = core_swap(packed1)
    total2 = keep2 + after(got2, packed1).astype(F32)
    own2 = own_ways(total2[:half])
    *pair2, sent2 = pair_ways(total2[half:])
    terms2 = (*own2, pair2[0], after(pair2[1], sent2))
    packed2 = pack(terms2, height)
    other2 = core_swap(packed2)
    total3 = keep3 + after(got3, packed2).astype(F32)
    own3 = own_ways(total3[:half])
    *pair3, sent3 = pair_ways(total3[half:])
    terms3 = (*own3, pair3[0], after(pair3[1], sent3))
    packed3 = pack(terms3, height)
    other3 = core_swap(packed3)
    blocks = [count // height for count in pieces]
    plan = ((0, 0, half // height, len(terms1)), (1, 0, blocks[0], len(terms2)), (1, blocks[0], blocks[1], len(terms3)))
    (result,) = local_call(
        functools.partial(finish_kernel, height, plan),
        [ancestor_rows[0], *terms1, other1, *terms2, other2, *terms3, other3],
        [(ancestor_rows.shape[1:], F32)],
        "finish",
    )
    return result[None]


def solution(mesh):
    def body(panel_blocks, factor_inverse, target_rows, owner_order, ancestor_rows):
        supernodes, panel_count, height, _ = panel_blocks.shape
        held = ancestor_rows.shape[0]
        paired = (
            mesh.shape["row"] == 4
            and mesh.shape["col"] == 8
            and panel_count == owner_order.shape[0] == 8
            and supernodes == 1
            and held == 1
            and height % 128 == 0
        )
        chosen = paired_body if paired else general_body
        return chosen(panel_blocks, factor_inverse, target_rows, owner_order, ancestor_rows)

    return jax.shard_map(
        body,
        mesh=mesh,
        in_specs=(
            P("col", None, "row", None),
            P("col", None, None),
            P(),
            P(),
            P("col", "row", None),
        ),
        out_specs=P("col", "row", None),
        check_vma=False,
    )
```

```python
import functools

import jax
import jax.numpy as jnp
from jax import lax
from jax.experimental import pallas as pl
from jax.experimental.pallas import tpu as pltpu
from jax.sharding import PartitionSpec as P

BF16 = jnp.bfloat16
F32 = jnp.float32
VMEM_LIMIT = 16 * 1024 * 1024
HINT = pl.CostEstimate(flops=1, bytes_accessed=1, transcendentals=0)


def solve_rows(blocks, factor_inverse):
    return jnp.einsum(
        "spiw,svw->spiv", blocks, factor_inverse, preferred_element_type=jnp.float32
    ).astype(jnp.bfloat16)


def pick_rows(products, own_targets, order_part):
    matched = own_targets[None, :, :] == order_part[:, None, None]
    places = lax.broadcasted_iota(jnp.int32, matched.shape, 2)
    position = jnp.sum(jnp.where(matched, places, 0), axis=2)
    present = jnp.any(matched, axis=2)
    supernode_ids = lax.broadcasted_iota(jnp.int32, position.shape, 1)
    chosen = products[supernode_ids, position]
    return jnp.where(present[:, :, None, None, None], chosen, jnp.zeros((), chosen.dtype))


def slot_select(targets, order_part, slot_count):
    matched = targets[None, :, :] == order_part[:, None, None]
    present = jnp.any(matched, axis=2)
    rank = jnp.cumsum(present.astype(jnp.int32), axis=1) - 1
    slot_ids = lax.broadcasted_iota(jnp.int32, (1, slot_count, 1), 1)
    selected = present[:, None, :] & (rank[:, None, :] == slot_ids)
    return selected.astype(jnp.float32)


def general_body(panel_blocks, factor_inverse, target_rows, owner_order, ancestor_rows):
    supernodes = panel_blocks.shape[0]
    panel_count = panel_blocks.shape[1]
    own_height = panel_blocks.shape[2]
    width = panel_blocks.shape[3]
    ancestors = owner_order.shape[0]
    col_devices = lax.axis_size("col")
    col_place = lax.axis_index("col")
    own_targets = lax.dynamic_slice_in_dim(target_rows, col_place * supernodes, supernodes, 0)
    own_solved = solve_rows(panel_blocks, factor_inverse)
    products = jnp.einsum(
        "spiw,sqmw->spiqm",
        own_solved,
        lax.all_gather(own_solved, "row", axis=2, tiled=True),
        preferred_element_type=jnp.float32,
    ).astype(jnp.bfloat16)
    block_ids = lax.broadcasted_iota(jnp.int32, (1, 1, 1, ancestors), 3)
    slot_count = (supernodes * panel_count + ancestors - 1) // ancestors
    chosen = pick_rows(products, own_targets, owner_order)
    own_select = slot_select(own_targets, owner_order, slot_count).astype(jnp.bfloat16)
    outgoing = jnp.einsum(
        "jas,jsiqw->jaiqw", own_select, chosen, preferred_element_type=jnp.float32
    ).astype(jnp.bfloat16)
    received = lax.all_to_all(outgoing, "col", split_axis=0, concat_axis=0, tiled=True)
    held_rows = ancestor_rows.shape[0]
    received = received.reshape(col_devices, held_rows, slot_count, own_height, panel_count, width)
    all_targets = target_rows.reshape(col_devices, supernodes, panel_count)
    held_order = lax.dynamic_slice_in_dim(owner_order, col_place * held_rows, held_rows, 0)
    all_select = jax.vmap(lambda targets: slot_select(targets, held_order, slot_count))(all_targets)
    all_onehot = (all_targets[:, :, :, None] == block_ids).astype(jnp.float32)
    column_map = jnp.einsum("ckas,csqb->ckaqb", all_select, all_onehot).astype(jnp.bfloat16)
    spread = jnp.einsum(
        "ckaqb,ckaiqw->kibw", column_map, received, preferred_element_type=jnp.float32
    )
    summed = spread.reshape(held_rows, own_height, ancestors * width)
    return ancestor_rows - summed


PAIR = (1, 0, 3, 2)
MIDDLE = (0, 2, 1, 3)
CORE, X_HOP, Y_HOP = 1, 2, 4
FIRST_HOP = (X_HOP, Y_HOP)
SECOND_HOP = (Y_HOP, X_HOP)


def row_swap(value, partner):
    return lax.ppermute(value, "row", list(enumerate(partner)))


def core_swap(value):
    return lax.ppermute(value, "col", [(i, i ^ CORE) for i in range(lax.axis_size("col"))])


def hop_swap(value, hops):
    return lax.ppermute(value, "col", [(i, i ^ hops[i & CORE]) for i in range(lax.axis_size("col"))])


def both_swap(value, partner, hops):
    cols = lax.axis_size("col")
    pairs = [(r * cols + c, partner[r] * cols + (c ^ hops[c & CORE])) for r in range(len(partner)) for c in range(cols)]
    return lax.ppermute(value, ("row", "col"), pairs)


def after(value, *others):
    return lax.optimization_barrier((value, *others))[0]


def dot_t(a, b):
    return lax.dot_general(a, b, (((1,), (1,)), ((), ())), preferred_element_type=F32)


def local_call(kernel, operands, shapes, name, scalars=0):
    whole = pl.BlockSpec(memory_space=pltpu.VMEM)
    return pl.pallas_call(
        kernel,
        in_specs=[pl.BlockSpec(memory_space=pltpu.SMEM)] * scalars + [whole] * (len(operands) - scalars),
        out_specs=[whole] * len(shapes),
        out_shape=[jax.ShapeDtypeStruct(shape, dtype) for shape, dtype in shapes],
        cost_estimate=HINT,
        compiler_params=pltpu.CompilerParams(vmem_limit_bytes=VMEM_LIMIT),
        name=name,
    )(*operands)


def core_index():
    return lax.axis_index("col") & CORE


def aligned(start, unit):
    return pl.ds(pl.multiple_of(start * unit, unit), unit)


def solve_kernel(other, panel_ref, inverse_ref, out_ref):
    part = 1 - core_index() if other else core_index()
    rows = aligned(part, out_ref.shape[0])
    out_ref[...] = dot_t(panel_ref[rows, :], inverse_ref[...]).astype(BF16)


def join_kernel(rest_ref, got_ref, *outs):
    width = rest_ref.shape[1]
    core = core_index()
    half = outs[0].shape[0]
    for out, first in zip(outs, (0, 0, half - outs[2].shape[0])):
        rows = pl.ds(first, out.shape[0])
        out[:, aligned(core, width)] = rest_ref[rows, :]
        out[:, aligned(1 - core, width)] = got_ref[rows, :]


def slot_masks():
    core = core_index()
    hop = jnp.where(core == 0, FIRST_HOP[0], FIRST_HOP[1])
    next_hop = jnp.where(core == 0, SECOND_HOP[0], SECOND_HOP[1])
    return [jnp.bitwise_xor(chip, side) for chip in (0, next_hop, hop, X_HOP | Y_HOP) for side in (0, CORE)]


def pick_own_kernel(height, order_ref, rest_ref, give_ref, got_ref, got_rest_ref, out_ref):
    col, core = lax.axis_index("col"), core_index()
    half, width = rest_ref.shape
    for place, mask in enumerate(slot_masks()):
        start = order_ref[jnp.bitwise_xor(col, mask)] * height
        rows = pl.ds(place * height, height)
        inside = start // half == core
        source = pl.ds(pl.multiple_of(start % half, height), height)
        for wanted, mine, other in ((inside, rest_ref, got_ref), (jnp.logical_not(inside), give_ref, got_rest_ref)):

            @pl.when(wanted)
            def _():
                out_ref[rows, aligned(core, width)] = mine[source, :]
                out_ref[rows, aligned(1 - core, width)] = other[source, :]


def pick_pair_kernel(height, valid, order_ref, *refs):
    pieces = len(valid)
    out_ref = refs[-1]
    col, core = lax.axis_index("col"), core_index()
    half = sum(count for _, count in valid)
    for place, mask in enumerate(slot_masks()):
        start = order_ref[jnp.bitwise_xor(col, mask)] * height
        rows = pl.ds(place * height, height)
        inside = start // half == core
        within = start % half
        for number in range(2 * pieces):
            ref = refs[number]
            skip, count = valid[number % pieces]
            first = sum(c for _, c in valid[: number % pieces])
            here = jnp.logical_and(within >= first, within < first + count)
            first = first - skip
            wanted = inside if number < pieces else jnp.logical_not(inside)

            @pl.when(jnp.logical_and(here, wanted))
            def _():
                out_ref[rows, :] = ref[pl.ds(pl.multiple_of(within - first, height), height), :]


def product_kernel(count, *refs):
    x_ref, keep_ref, send_ref = refs[count:]
    for number, a_ref in enumerate(refs[:count]):
        tile = a_ref.shape[0] // 2
        rows = pl.ds(number * tile, tile)
        keep_ref[rows, :] = dot_t(a_ref[:tile, :], x_ref[...])
        send_ref[rows, :] = dot_t(a_ref[tile:, :], x_ref[...]).astype(BF16)


def products(a, x):
    shape = (sum(part.shape[0] for part in a) // 2, x.shape[0])
    return local_call(functools.partial(product_kernel, len(a)), [*a, x], [(shape, F32), (shape, BF16)], "products")


def own_ways(total):
    half = total.shape[0] // 2
    return total[:half], hop_swap(total[half:].astype(BF16), SECOND_HOP)


def pair_ways(total):
    half = total.shape[0] // 2
    total = total.astype(BF16)
    return row_swap(total[:half], PAIR), both_swap(total[half:], PAIR, SECOND_HOP), total


def pack(terms, height):
    return jnp.concatenate([term[height : 2 * height].astype(BF16) for term in terms], axis=0)


def finish_kernel(height, plan, anc_ref, *refs):
    out_ref = refs[-1]
    row, core = lax.axis_index("row"), core_index()
    width = 4 * height
    half = out_ref.shape[1] // 2
    base = jnp.bitwise_or((row & 1) * 2, row >> 1)
    position = 0
    tile = out_ref.shape[0]
    rows = aligned(pl.program_id(0), tile)
    for which, first, count, terms in plan:
        mine = refs[position : position + terms]
        other = refs[position + terms]
        position += terms + 1
        for returned, wanted in enumerate((range(2), range(2, terms))):
            at = jnp.bitwise_xor(base, which + 2 * returned)
            for block in range(count):
                source = pl.ds(block * height, height)
                for side in range(2):
                    if side:
                        tiles = [other[aligned(k * (height // tile) + pl.program_id(0), tile), source] for k in wanted]
                    else:
                        tiles = [mine[k][rows, source] for k in wanted]
                    total = sum(tile.astype(F32) for tile in tiles)
                    place = (1 - core if side else core) * half + (first + block) * width + at * height
                    place = pl.ds(pl.multiple_of(place, height), height)
                    out_ref[:, place] = anc_ref[rows, place] - total


def paired_body(panel_blocks, factor_inverse, target_rows, owner_order, ancestor_rows):
    _, panel_count, height, width = panel_blocks.shape
    rows = panel_count * height
    panel = panel_blocks.reshape(rows, width)
    half = rows // 2
    pieces = (2 * height, half - 2 * height)
    valid = [(0, count) for count in pieces]

    inverse = factor_inverse[0]
    half_shape = [((half, width), BF16)]
    (give,) = local_call(functools.partial(solve_kernel, True), [panel, inverse], half_shape, "solve")
    got = core_swap(give)
    (rest,) = local_call(functools.partial(solve_kernel, False), [panel, after(inverse, give)], half_shape, "solve")
    got_rest = core_swap(rest)
    joined, *parts = local_call(
        join_kernel, [rest, got], [((count, 2 * width), BF16) for count in (half, *pieces)], "join"
    )
    pair = [row_swap(part, PAIR) for part in parts]
    (a_own,) = local_call(
        functools.partial(pick_own_kernel, height),
        [owner_order, rest, give, got, got_rest],
        [((rows, 2 * width), BF16)],
        "pick_own",
        scalars=1,
    )
    first = row_swap(after(joined, a_own), MIDDLE)
    second = [row_swap(after(pair[0], a_own), MIDDLE), row_swap(pair[1], MIDDLE)]
    pair_b = core_swap(pair[0])
    (a_pair,) = local_call(
        functools.partial(pick_pair_kernel, height, valid),
        [owner_order, *pair, pair_b, core_swap(after(pair[1], pair_b))],
        [((rows, 2 * width), BF16)],
        "pick_pair",
        scalars=1,
    )
    keep_own, send = products([a_own], first)
    got_own = hop_swap(send, FIRST_HOP)
    keep_pair, send = products([after(a_pair, keep_own)], first)
    got_pair = hop_swap(send, FIRST_HOP)
    keep2, send = products([a_own, a_pair], after(second[0], keep_pair))
    got2 = hop_swap(send, FIRST_HOP)
    own1 = own_ways(keep_own + after(got_own, keep2).astype(F32))
    *pair1, sent1 = pair_ways(keep_pair + after(got_pair, own1[0]).astype(F32))
    keep3, send = products([a_own, a_pair], after(second[1], keep2))
    got3 = hop_swap(send, FIRST_HOP)
    terms1 = (*own1, pair1[0], after(pair1[1], keep3))
    packed1 = pack(terms1, height)
    other1 = core_swap(packed1)
    total2 = keep2 + after(got2, packed1).astype(F32)
    own2 = own_ways(total2[:half])
    *pair2, sent2 = pair_ways(total2[half:])
    terms2 = (*own2, pair2[0], after(pair2[1], sent2))
    packed2 = pack(terms2, height)
    other2 = core_swap(packed2)
    total3 = keep3 + after(got3, packed2).astype(F32)
    own3 = own_ways(total3[:half])
    *pair3, sent3 = pair_ways(total3[half:])
    terms3 = (*own3, pair3[0], after(pair3[1], sent3))
    packed3 = pack(terms3, height)
    other3 = core_swap(packed3)
    blocks = [count // height for count in pieces]
    plan = ((0, 0, half // height, len(terms1)), (1, 0, blocks[0], len(terms2)), (1, blocks[0], blocks[1], len(terms3)))
    operands = [ancestor_rows[0], *terms1, other1, *terms2, other2, *terms3, other3]
    columns = ancestor_rows.shape[2]
    result = pl.pallas_call(
        functools.partial(finish_kernel, height, plan),
        grid=(2,),
        in_specs=[pl.BlockSpec(memory_space=pltpu.VMEM)] * len(operands),
        out_specs=pl.BlockSpec((height // 2, columns), lambda i: (i, 0)),
        out_shape=jax.ShapeDtypeStruct((height, columns), F32),
        cost_estimate=HINT,
        compiler_params=pltpu.CompilerParams(vmem_limit_bytes=VMEM_LIMIT),
        name="finish",
    )(*operands)
    return result[None]


def solution(mesh):
    def body(panel_blocks, factor_inverse, target_rows, owner_order, ancestor_rows):
        supernodes, panel_count, height, _ = panel_blocks.shape
        held = ancestor_rows.shape[0]
        paired = (
            mesh.shape["row"] == 4
            and mesh.shape["col"] == 8
            and panel_count == owner_order.shape[0] == 8
            and supernodes == 1
            and held == 1
            and height % 128 == 0
        )
        chosen = paired_body if paired else general_body
        return chosen(panel_blocks, factor_inverse, target_rows, owner_order, ancestor_rows)

    return jax.shard_map(
        body,
        mesh=mesh,
        in_specs=(
            P("col", None, "row", None),
            P("col", None, None),
            P(),
            P(),
            P("col", "row", None),
        ),
        out_specs=P("col", "row", None),
        check_vma=False,
    )
```
